32 devices in a mesh: replica: 2 (over x), owner: 16 (over z, y, core).
Axes of the slice: x: 2, y: 2, z: 4, core: 2. Of those that a mesh axis runs over, the one named last changes fastest.
Arguments:
- hidden: bfloat16 [4096, 5120], P(('replica', 'owner')), parts along dimension 0, may hold values from -6 to 6
- base_weight: bfloat16 [5120, 1024], replicated, may hold values from -0.078125 to 0.078125
- factor_down: bfloat16 [16, 64, 5120], P('owner'), may hold values from -0.078125 to 0.078125
- factor_up: bfloat16 [16, 64, 1024], P('owner'), may hold values from -0.75 to 0.75
- group_variants: int32 [32, 4], P(('replica', 'owner')), parts along dimension 0, may hold values from 0 to 15, all different within a row
- row_choice: int32 [4096], P(('replica', 'owner')), parts along dimension 0, may hold values from 0 to 3
- slot_of: int32 [16], replicated, may hold values from 0 to 15, each once
Outputs:
- adapted: bfloat16 [4096, 1024], P(('replica', 'owner')), parts along dimension 0
The draws below stay inside these ranges and needn't reach their ends.
There are 2 independent parts, one for each index of `replica`. The reference program is written for one: setup_inputs(seed, part) draws one part's arguments, and reference() takes and returns one part's arrays. A program takes and returns all parts, laid end to end along the dimension named above; an argument that names none is the same for every part. Nothing has to cross between parts.
Inputs may be any that keep to these rules, and one draw needn't show every extreme that they name: `group_variants`: each group lists 4 different variants; every variant is listed by some group of each replica. `slot_of`: each storage slot is taken by exactly one variant.
All inputs are finite; a program needn't handle non-finite values.
Results may differ from the reference program's by a relative error of at most 0.0041.
Values may be sent and summed in bfloat16 or wider, within the bound.
No kernel may reach another device: no remote copies, remote signals or barrier semaphores. Data moves between devices by JAX's collectives and lax.ppermute only.
A program may use at most 64 MiB of HBM per device.

```python
import jax
import jax.numpy as jnp
from jax import lax

D = 5120
RANK = 64
VAR_GROUP = 4
ROWS_DEV = 128
QW = 1024
GROUPS = 16
VARIANTS = 16
ROWS = 2048


def with_ends(result, key, least, largest):
    longest = result.shape.index(max(result.shape))
    spots = []
    for shift in (0, 1):
        where = [jax.random.randint(jax.random.fold_in(key, axis), (), 0, length) for axis, length in enumerate(result.shape)]
        where[longest] = (where[longest] + shift) % result.shape[longest]
        spots.append(tuple(where))
    return result.at[spots[0]].set(least).at[spots[1]].set(largest)


def shard_levels(own_key, dims, pieces, least, largest):
    def one(position, parts):
        draws = jax.random.uniform(jax.random.fold_in(jax.random.fold_in(own_key, 6), position), (parts,), jnp.float32, least / len(pieces), largest / len(pieces))
        return jnp.repeat(jnp.exp(draws), dims[position] // parts).reshape((-1,) + (1,) * (len(dims) - position - 1))

    gain = one(*pieces[0])
    for cut in pieces[1:]:
        gain = gain * one(*cut)
    return gain


def distinct(stream_key, rows, amount, top, lift):
    ranking = jax.random.permutation(jax.random.fold_in(stream_key, 1), amount)
    pull = ranking
    for power in range(3):
        pull = pull * pull // amount
    pull = pull * lift // amount
    lots = jax.random.randint(jax.random.fold_in(stream_key, 2), (rows, amount), 0, 4096) + pull
    fixed_rows = jax.random.permutation(jax.random.fold_in(stream_key, 3), rows)[jnp.arange(amount) % rows]
    lots = jnp.where(jnp.arange(rows)[:, None] == fixed_rows[None, :], 1 << 14, lots)
    priority = lots * amount + jnp.arange(amount)
    return lax.top_k(priority.astype(jnp.int32), top)[1].astype(jnp.int32)


def scatter_about(rng, extent, scale, most, split=(), kind=jnp.bfloat16):
    entries = jax.random.normal(rng, extent, jnp.float32) * scale
    if len(split) > 0:
        entries = shard_levels(rng, extent, split, -0.22, 0.18) * entries
    return jnp.clip(entries, min=-most, max=most).astype(kind)


def setup_inputs(seed: int = 0, part: int = 0) -> dict:
    key_list = jax.random.split(jax.random.key(seed), 8)
    part_splits = jax.random.split(jax.random.fold_in(key_list[7], part), 8)
    return {
        "hidden": scatter_about(part_splits[0], (ROWS, D), 1.0, 6.0, ((0, 16),)),
        "base_weight": scatter_about(key_list[1], (D, QW), D ** -0.5, 0.078125),
        "factor_down": scatter_about(key_list[2], (VARIANTS, RANK, D), D ** -0.5, 0.078125, ((0, 16),)),
        "factor_up": scatter_about(key_list[3], (VARIANTS, RANK, QW), RANK ** -0.5, 0.75, ((0, 16),)),
        "group_variants": distinct(part_splits[4], GROUPS, VARIANTS, VAR_GROUP, 4096),
        "row_choice": with_ends(jax.random.randint(part_splits[5], (ROWS,), 0, VAR_GROUP), jax.random.fold_in(part_splits[5], 1), 0, VAR_GROUP - 1).astype(jnp.int32),
        "slot_of": jax.random.permutation(key_list[6], VARIANTS).astype(jnp.int32),
    }


def reference(hidden, base_weight, factor_down, factor_up, group_variants, row_choice, slot_of):
    base = jnp.dot(hidden, base_weight, preferred_element_type=jnp.float32)
    slots = jnp.take(slot_of, group_variants, axis=0).astype(jnp.int32)
    grouped_rows = hidden.reshape(-1, ROWS_DEV, D)
    grouped_choice = row_choice.reshape(-1, ROWS_DEV)

    def one_group(items):
        rows, chosen, own = items
        downs = jnp.take(factor_down, own, axis=0).astype(jnp.float32)
        ups = jnp.take(factor_up, own, axis=0).astype(jnp.float32)
        every_z = jnp.einsum("rd,cjd->rcj", rows.astype(jnp.float32), downs)
        select = (chosen[:, None] == jnp.arange(VAR_GROUP, dtype=jnp.int32)[None, :]).astype(jnp.float32)
        picked = jnp.einsum("rcj,rc->rj", every_z, select).astype(jnp.bfloat16)
        masked = select[:, :, None] * picked.astype(jnp.float32)[:, None, :]
        return jnp.einsum("rcj,cjq->rq", masked, ups)

    delta = lax.map(one_group, (grouped_rows, grouped_choice, slots)).reshape(-1, QW)
    return (base + delta).astype(jnp.bfloat16)
```

```python
import jax
import jax.numpy as jnp
from jax import lax
from jax.sharding import PartitionSpec as P


def body(hidden, base_weight, factor_down, factor_up, group_variants, row_choice, slot_of):
    owners = lax.axis_size("owner")
    replicas = lax.axis_size("replica")
    assert replicas == 2 and owners % 4 == 0 and owners <= 256
    planes = owners // 4
    rows, width = hidden.shape
    rank = factor_down.shape[1]
    qwidth = factor_up.shape[2]
    half, qhalf = width // 2, qwidth // 2
    x = lax.axis_index("replica")
    here = lax.axis_index("owner")
    plane, column, core = here // 4, here // 2 % 2, here % 2

    def by_owner(value, flip):
        return lax.ppermute(value, "owner", [(i, i ^ flip) for i in range(owners)])

    def across(value, flip):
        pairs = [
            (r * owners + i, (1 - r) * owners + (i ^ flip)) for r in range(2) for i in range(owners)
        ]
        return lax.ppermute(value, ("replica", "owner"), pairs)

    def to_x(value):
        return across(value, 0)

    def to_y(value):
        return by_owner(value, 2)

    def to_d(value):
        return across(value, 2)

    def to_core(value):
        return by_owner(value, 1)

    variants = jnp.arange(slot_of.shape[0], dtype=jnp.int32)
    listed = jnp.sum(
        jnp.where(group_variants[0][:, None] == variants[None, :], slot_of[None, :], 0), axis=1
    )
    places = jnp.arange(listed.shape[0], dtype=jnp.int32)
    slot = jnp.sum(jnp.where(row_choice[:, None] == places[None, :], listed[None, :], 0), axis=1)
    tag = jnp.broadcast_to(slot.astype(jnp.bfloat16)[:, None], (rows, 128))

    unit = jnp.concatenate(
        [
            lax.dynamic_slice_in_dim(factor_down[0], x * half, half, axis=1),
            lax.dynamic_slice_in_dim(factor_up[0], x * qhalf, qhalf, axis=1),
        ],
        axis=1,
    )
    units = [unit] + [by_owner(unit, 4 * s) for s in range(1, planes)]

    mine = jnp.concatenate([lax.dynamic_slice_in_dim(hidden, x * half, half, axis=1), tag], axis=1)
    other = jnp.concatenate(
        [lax.dynamic_slice_in_dim(hidden, (1 - x) * half, half, axis=1), tag], axis=1
    )
    blocks = [mine, to_x(other), to_y(mine), to_d(other)]

    base = jnp.dot(hidden, base_weight, preferred_element_type=jnp.float32)

    downs = [u[:, :half] for u in units]
    downs_other = [to_core(d) for d in downs]
    ups = jnp.concatenate([u[:, half:] for u in units], axis=0)
    ups = [ups, to_x(ups), to_y(ups), to_d(ups)]
    ups_other = [to_core(u) for u in ups]

    hid = jnp.concatenate([b[:, :half] for b in blocks], axis=0)
    tags = jnp.concatenate([b[:, half : half + 1] for b in blocks], axis=0).astype(jnp.int32)
    part = jnp.zeros((4 * rows, rank), jnp.float32)
    for s in range(planes):
        first = (plane ^ s) * 4 + column * 2
        for pair, which in ((downs[s], core), (downs_other[s], 1 - core)):
            z = lax.dot_general(
                hid, pair, (((1,), (1,)), ((), ())), preferred_element_type=jnp.float32
            )
            part = jnp.where(tags == first + which, z, part)
    part = part.reshape(4, rows, rank)
    total = part[0] + to_x(part[1]) + to_y(part[2]) + to_d(part[3])
    z = total.astype(jnp.bfloat16)

    def spread(col, cor):
        ids = jnp.stack([(plane ^ s) * 4 + col * 2 + cor for s in range(planes)])
        keep = slot[:, None, None] == ids[None, :, None]
        return jnp.where(keep, z[:, None, :], 0).reshape(rows, planes * rank)

    own_half = jnp.zeros((rows, qhalf), jnp.float32)
    oth_half = jnp.zeros((rows, qhalf), jnp.float32)
    for held, cor in ((ups, core), (ups_other, 1 - core)):
        a, b = spread(column, cor), spread(1 - column, cor)
        own_half += jnp.dot(a, held[0], preferred_element_type=jnp.float32)
        oth_half += jnp.dot(a, held[1], preferred_element_type=jnp.float32)
        own_half += jnp.dot(b, held[2], preferred_element_type=jnp.float32)
        oth_half += jnp.dot(b, held[3], preferred_element_type=jnp.float32)
    delta = jnp.where(
        x == 0,
        jnp.concatenate([own_half, oth_half], axis=1),
        jnp.concatenate([oth_half, own_half], axis=1),
    )
    return (base + delta).astype(jnp.bfloat16)


def solution(mesh):
    return jax.shard_map(
        body,
        mesh=mesh,
        in_specs=(
            P(("replica", "owner"), None),
            P(),
            P("owner", None, None),
            P("owner", None, None),
            P(("replica", "owner"), None),
            P(("replica", "owner")),
            P(),
        ),
        out_specs=P(("replica", "owner"), None),
        check_vma=False,
    )
```

```python
import functools

import jax
import jax.numpy as jnp
from jax import lax
from jax.experimental import pallas as pl
from jax.experimental.pallas import tpu as pltpu
from jax.sharding import PartitionSpec as P

TAG = 128
VMEM = pl.BlockSpec(memory_space=pltpu.VMEM)
SMEM = pl.BlockSpec(memory_space=pltpu.SMEM)


def call(kernel, out, operands, scalars=0, flops=0, scratch=()):
    moved = sum(o.size * o.dtype.itemsize for o in operands)
    moved += sum(o.size * o.dtype.itemsize for o in jax.tree.leaves(out))
    return pl.pallas_call(
        kernel,
        out_shape=out,
        in_specs=[SMEM] * scalars + [VMEM] * (len(operands) - scalars),
        out_specs=jax.tree.map(lambda _: VMEM, out),
        scratch_shapes=scratch,
        cost_estimate=pl.CostEstimate(flops=flops, bytes_accessed=moved, transcendentals=0),
        compiler_params=pltpu.CompilerParams(vmem_limit_bytes=48 << 20),
    )(*operands)


def slice_factors(place, down, up, own, swapped):
    quarter, qhalf = swapped.shape[1], own.shape[1] - swapped.shape[1]
    x, column = place[0], place[2]
    mine, theirs = x * 2 + column, x * 2 + 1 - column
    own[:, :quarter] = down[0, :, pl.ds(pl.multiple_of(mine * quarter, 128), quarter)]
    own[:, quarter:] = up[0, :, pl.ds(pl.multiple_of(x * qhalf, 128), qhalf)]
    swapped[...] = down[0, :, pl.ds(pl.multiple_of(theirs * quarter, 128), quarter)]


def slice_rows(place, hidden, slot, *outs):
    quarter = outs[0].shape[1] - TAG
    x, column = place[0], place[2]
    tag = jnp.broadcast_to(slot[...], (slot.shape[0], TAG)).astype(jnp.float32).astype(jnp.bfloat16)
    parts = (x * 2 + column, (1 - x) * 2 + column, x * 2 + 1 - column, (1 - x) * 2 + 1 - column)
    for part, out in zip(parts, outs):
        out[:, :quarter] = hidden[:, pl.ds(pl.multiple_of(part * quarter, 128), quarter)]
        out[:, quarter:] = tag


def ids_of(plane, column, core, first, count, rank):
    lane = lax.broadcasted_iota(jnp.int32, (1, count * rank), 1)
    return ((plane ^ (first + lane // rank)) * 4) + column * 2 + core


def sum_z(flipped, units, merged, place, *refs):
    plane, column, core = place[1], place[2], place[3]
    column = 1 - column if flipped else column
    blocks, refs = refs[:8], refs[8:]
    held, refs = refs[: units + merged], refs[units + merged :]
    *before, out, hid = refs
    rows, quarter = blocks[0].shape[0], blocks[0].shape[1] - TAG
    rank = held[0].shape[0]
    for i, block in enumerate(blocks):
        hid[i * rows : (i + 1) * rows, :] = block[:, :quarter]
    tags = [b[:, quarter : quarter + 1].astype(jnp.float32).astype(jnp.int32) for b in blocks]
    some = min(units, 4)
    for first in range(0, units, some):
        parts = [h[:, :quarter] for h in held[first : first + some]]
        if merged:
            parts[-1] = parts[-1] + held[units][:, :quarter]
        z = lax.dot_general(
            hid[...],
            jnp.concatenate(parts, axis=0),
            (((1,), (1,)), ((), ())),
            preferred_element_type=jnp.float32,
        )
        ids = ids_of(plane, column, core, first, some, rank)
        for i in range(8):
            kept = jnp.where(tags[i] == ids, z[i * rows : (i + 1) * rows, :], 0.0)
            kept = sum(kept[:, j : j + 128] for j in range(0, some * rank, 128))
            if first:
                out[i] += kept
            elif before:
                out[i] = before[0][i] + kept
            else:
                out[i] = kept


def add_up(planes, place, base, mine, total, swapped, *refs):
    *held, out = refs
    x, plane, column, core = place[0], place[1], place[2], place[3]
    rows, quarter = mine.shape[0], mine.shape[1] - TAG
    rank = total.shape[1] // 2
    qhalf = held[0].shape[1]
    tag = mine[:, quarter : quarter + 1].astype(jnp.float32).astype(jnp.int32)
    both = total[...] + swapped[...]
    z = (both[:, :rank] + both[:, rank:]).astype(jnp.bfloat16).astype(jnp.float32)
    some = min(planes, 4)
    spread = jnp.concatenate([z] * some, axis=1)
    near = jnp.zeros((rows, qhalf), jnp.float32)
    far = jnp.zeros((rows, qhalf), jnp.float32)
    for first in range(0, planes, some):
        span = slice(first * rank, (first + some) * rank)
        for c in range(2):
            for y in range(2):
                ids = ids_of(
                    plane, 1 - column if y else column, 1 - core if c else core, first, some, rank
                )
                picked = jnp.where(tag == ids, spread, 0.0).astype(jnp.bfloat16)
                near += jnp.dot(
                    picked, held[c * 4 + y * 2][span, :], preferred_element_type=jnp.float32
                )
                far += jnp.dot(
                    picked, held[c * 4 + y * 2 + 1][span, :], preferred_element_type=jnp.float32
                )
    at_near = pl.multiple_of(x * qhalf, 128)
    at_far = pl.multiple_of((1 - x) * qhalf, 128)
    out[:, pl.ds(at_near, qhalf)] = (base[:, pl.ds(at_near, qhalf)] + near).astype(out.dtype)
    out[:, pl.ds(at_far, qhalf)] = (base[:, pl.ds(at_far, qhalf)] + far).astype(out.dtype)


def body(hidden, base_weight, factor_down, factor_up, group_variants, row_choice, slot_of):
    owners = lax.axis_size("owner")
    assert lax.axis_size("replica") == 2 and owners % 4 == 0 and owners <= 256
    planes = owners // 4
    rows, width = hidden.shape
    rank = factor_down.shape[1]
    qwidth = factor_up.shape[2]
    quarter, qhalf = width // 4, qwidth // 2
    here = lax.axis_index("owner")
    place = jnp.stack([lax.axis_index("replica"), here // 4, (here // 2) % 2, here % 2])

    def by_owner(value, flip):
        return lax.ppermute(value, "owner", [(i, i ^ flip) for i in range(owners)])

    def between(value, pairs):
        return lax.ppermute(
            value, "owner", [(a * 4 + i, b * 4 + i) for a, b in pairs for i in range(4)]
        )

    def across(value, flip):
        pairs = [
            (r * owners + i, (1 - r) * owners + (i ^ flip)) for r in range(2) for i in range(owners)
        ]
        return lax.ppermute(value, ("replica", "owner"), pairs)

    def to_x(value):
        return across(value, 0)

    def to_y(value):
        return by_owner(value, 2)

    def to_d(value):
        return across(value, 2)

    def to_core(value):
        return by_owner(value, 1)

    def along(unit):
        if planes != 4:
            return [unit] + [by_owner(unit, 4 * s) for s in range(1, planes)]
        second = by_owner(unit, 8)
        first = by_owner(unit, 4)
        middle = between(unit, [(1, 2), (2, 1)])
        ends = between(second, [(1, 0), (2, 3)])
        return [unit, first, second, middle, ends]

    merged = 1 if planes == 4 else 0
    bf16, f32 = jnp.bfloat16, jnp.float32

    own, swapped = call(
        slice_factors,
        (
            jax.ShapeDtypeStruct((rank, quarter + qhalf), bf16),
            jax.ShapeDtypeStruct((rank, quarter), bf16),
        ),
        (place, factor_down, factor_up),
        scalars=1,
    )
    partner = to_y(swapped)
    a_units = along(own)
    b_units = along(partner)

    variants = jnp.arange(slot_of.shape[0], dtype=jnp.int32)
    listed = jnp.sum(
        jnp.where(group_variants[0][:, None] == variants[None, :], slot_of[None, :], 0), axis=1
    )
    places = jnp.arange(listed.shape[0], dtype=jnp.int32)
    slot = jnp.sum(jnp.where(row_choice[:, None] == places[None, :], listed[None, :], 0), axis=1)
    mine, for_x, for_y, for_d = call(
        slice_rows,
        (jax.ShapeDtypeStruct((rows, quarter + TAG), bf16),) * 4,
        (place, hidden, slot[:, None]),
        scalars=1,
    )
    blocks = [mine, to_x(for_x), to_y(for_y), to_d(for_d)]
    blocks = blocks + [to_core(b) for b in blocks]

    base = jnp.dot(hidden, base_weight, preferred_element_type=f32)

    ups = [u[:, quarter:] for u in a_units]
    if merged:
        ups = ups[:3] + [ups[3] + ups[4]]
    ups = jnp.concatenate(ups, axis=0)
    ups = [ups, to_x(ups), to_y(ups), to_d(ups)]
    ups = ups + [to_core(u) for u in ups]

    part_shape = jax.ShapeDtypeStruct((8, rows, 2 * rank), f32)
    scratch = [pltpu.VMEM((8 * rows, quarter), bf16)]
    flops = 2 * 8 * rows * quarter * planes * rank
    part = call(
        functools.partial(sum_z, False, planes, merged),
        part_shape,
        (place, *blocks, *a_units),
        scalars=1,
        flops=flops,
        scratch=scratch,
    )
    part = call(
        functools.partial(sum_z, True, planes, merged),
        part_shape,
        (place, *blocks, *b_units, part),
        scalars=1,
        flops=flops,
        scratch=scratch,
    )
    part = part.reshape(2, 4, rows, 2 * rank)
    total = part[:, 0] + to_x(part[:, 1]) + to_y(part[:, 2]) + to_d(part[:, 3])
    return call(
        functools.partial(add_up, planes),
        jax.ShapeDtypeStruct((rows, qwidth), bf16),
        (place, base, mine, total[0], to_core(total[1]), *ups),
        scalars=1,
        flops=2 * rows * owners * rank * qwidth,
    )


def solution(mesh):
    return jax.shard_map(
        body,
        mesh=mesh,
        in_specs=(
            P(("replica", "owner"), None),
            P(),
            P("owner", None, None),
            P("owner", None, None),
            P(("replica", "owner"), None),
            P(("replica", "owner")),
            P(),
        ),
        out_specs=P(("replica", "owner"), None),
        check_vma=False,
    )
```

```python
import functools

import jax
import jax.numpy as jnp
from jax import lax
from jax.experimental import pallas as pl
from jax.experimental.pallas import tpu as pltpu
from jax.sharding import PartitionSpec as P

TAG = 128
ORDER = {
    "Y": ("P", "A1"),
    "A3": ("A1", "P"),
    "D": ("X", "A2"),
    "B1": ("A3", "Y"),
    "B3": ("A3",),
    "base": ("P",),
    "A4": ("base",),
    "B4": ("A4",),
    "C1": ("A4", "B1", "B2"),
    "C2": ("A4", "B1", "B2"),
}
VMEM = pl.BlockSpec(memory_space=pltpu.VMEM)
SMEM = pl.BlockSpec(memory_space=pltpu.SMEM)
HBM = pl.BlockSpec(memory_space=pltpu.HBM)


def call(kernel, out, operands, scalars=0, whole=0, flops=0, scratch=()):
    operands = list(operands)
    if whole:
        operands[-whole:] = [
            pltpu.with_memory_space_constraint(o, pltpu.HBM) for o in operands[-whole:]
        ]
    moved = sum(o.size * o.dtype.itemsize for o in operands)
    return pl.pallas_call(
        kernel,
        out_shape=out,
        in_specs=[SMEM] * scalars + [VMEM] * (len(operands) - scalars - whole) + [HBM] * whole,
        out_specs=jax.tree.map(lambda _: VMEM, out),
        scratch_shapes=scratch,
        cost_estimate=pl.CostEstimate(flops=flops, bytes_accessed=moved, transcendentals=0),
        compiler_params=pltpu.CompilerParams(vmem_limit_bytes=(16 if whole else 48) << 20),
    )(*operands)


def slices(place, down, up, hbm_variants, hbm_slots, hbm_choice, hidden, *refs):
    swapped, own, *outs, variants, slot_of, choice, sems = refs
    quarter, qhalf = swapped.shape[1], own.shape[1] - swapped.shape[1]
    rows = outs[0].shape[0]
    x, column = place[0], place[2]

    def columns(part, width):
        return pl.ds(pl.multiple_of(part * width, 128), width)

    parts = (x * 2 + column, (1 - x) * 2 + column, x * 2 + 1 - column, (1 - x) * 2 + 1 - column)
    pairs = [
        (hbm_variants, variants),
        (hbm_slots, slot_of),
        (hbm_choice, choice),
        (down.at[0, :, columns(parts[2], quarter)], swapped),
        (down.at[0, :, columns(parts[0], quarter)], own.at[:, :quarter]),
        (up.at[0, :, columns(x, qhalf)], own.at[:, quarter:]),
    ]
    pairs += [
        (hidden.at[:, columns(part, quarter)], out.at[:, :quarter])
        for part, out in zip(parts, outs)
    ]
    copies = [pltpu.make_async_copy(a, b, sems.at[i]) for i, (a, b) in enumerate(pairs)]
    for copy in copies:
        copy.start()
    for copy in copies[:3]:
        copy.wait()
    slot = jnp.zeros((1, rows), jnp.int32)
    for k in range(variants.shape[1]):
        slot = jnp.where(choice[...] == k, slot_of[variants[0, k]], slot)
    diagonal = lax.broadcasted_iota(jnp.int32, (rows, rows), 0) == lax.broadcasted_iota(
        jnp.int32, (rows, rows), 1
    )
    column = jnp.sum(jnp.where(diagonal, slot.astype(jnp.float32), 0.0), axis=1, keepdims=True)
    tag = jnp.broadcast_to(column, (rows, TAG)).astype(jnp.bfloat16)
    for out in outs:
        out[:, quarter:] = tag
    for copy in copies[3:]:
        copy.wait()


def ids_of(plane, column, core, first, count, rank):
    lane = lax.broadcasted_iota(jnp.int32, (1, count * rank), 1)
    return ((plane ^ (first + lane // rank)) * 4) + column * 2 + core


def sum_z(flipped, units, merged, place, *refs):
    plane, column, core = place[1], place[2], place[3]
    column = 1 - column if flipped else column
    blocks, refs = refs[:6], refs[6:]
    held, refs = refs[: units + merged], refs[units + merged :]
    *refs, hid = refs
    before, outs = (refs[:1], refs[1:]) if flipped else ((), refs)
    rows, quarter = blocks[0].shape[0], blocks[0].shape[1] - TAG
    rank = held[0].shape[0]
    tags = []
    for block in blocks:
        for first in range(0, block.shape[0], rows):
            span = slice(first, first + rows)
            hid[len(tags) * rows : (len(tags) + 1) * rows, :] = block[span, :quarter]
            tag = block[span, quarter : quarter + 1]
            tags.append(tag.astype(jnp.float32).astype(jnp.int32))
    some = min(units, 4)
    sums = [before[0][i] if before else None for i in range(8)]
    for first in range(0, units, some):
        parts = [h[:, :quarter] for h in held[first : first + some]]
        if merged:
            parts[-1] = parts[-1] + held[units][:, :quarter]
        z = lax.dot_general(
            hid[...],
            jnp.concatenate(parts, axis=0),
            (((1,), (1,)), ((), ())),
            preferred_element_type=jnp.float32,
        )
        ids = ids_of(plane, column, core, first, some, rank)
        for i in range(8):
            kept = jnp.where(tags[i] == ids, z[i * rows : (i + 1) * rows, :], 0.0)
            kept = sum(kept[:, j : j + 128] for j in range(0, some * rank, 128))
            sums[i] = kept if sums[i] is None else sums[i] + kept
    for i in range(8):
        if flipped:
            outs[i % 4][i // 4] = sums[i]
        else:
            outs[0][i] = sums[i]


def add_up(planes, place, base, mine, theirs, z_here, z_x, z_y, z_d, *refs):
    *held, out, away = refs
    x, plane, column, core = place[0], place[1], place[2], place[3]
    rows, quarter = mine.shape[0], mine.shape[1] - TAG
    rank = z_here.shape[2] // 2
    qhalf = held[0].shape[1]
    tag = jnp.concatenate(
        [mine[:, quarter : quarter + 1], theirs[:rows, quarter : quarter + 1]], axis=0
    )
    tag = tag.astype(jnp.float32).astype(jnp.int32)
    both = [z_here[i] + z_x[i] + z_y[i] + z_d[i] for i in range(2)]
    z = jnp.concatenate([b[:, :rank] + b[:, rank:] for b in both], axis=0)
    z = z.astype(jnp.bfloat16).astype(jnp.float32)
    some = min(planes, 4)
    spread = jnp.concatenate([z] * some, axis=1)
    near = jnp.zeros((2 * rows, qhalf), jnp.float32)
    far = jnp.zeros((2 * rows, qhalf), jnp.float32)
    for first in range(0, planes, some):
        span = slice(first * rank, (first + some) * rank)
        for y in range(2):
            ids = ids_of(plane, 1 - column if y else column, core, first, some, rank)
            picked = jnp.where(tag == ids, spread, 0.0).astype(jnp.bfloat16)
            near += jnp.dot(picked, held[y * 2][span, :], preferred_element_type=jnp.float32)
            far += jnp.dot(picked, held[y * 2 + 1][span, :], preferred_element_type=jnp.float32)
    for half, value in ((x, near), (1 - x, far)):
        columns = pl.ds(pl.multiple_of(half * qhalf, 128), qhalf)
        out[:, columns] = base[:, columns] + value[:rows]
        away[:, columns] = value[rows:]


def add(here, came, out):
    out[...] = (here[...] + came[...]).astype(out.dtype)


def body(hidden, base_weight, factor_down, factor_up, group_variants, row_choice, slot_of):
    owners = lax.axis_size("owner")
    assert lax.axis_size("replica") == 2 and owners % 4 == 0 and owners <= 256
    planes = owners // 4
    rows, width = hidden.shape
    rank = factor_down.shape[1]
    qwidth = factor_up.shape[2]
    quarter, qhalf = width // 4, qwidth // 2
    here = lax.axis_index("owner")
    place = jnp.stack([lax.axis_index("replica"), here // 4, (here // 2) % 2, here % 2])

    def by_owner(value, flip):
        return lax.ppermute(value, "owner", [(i, i ^ flip) for i in range(owners)])

    def between(value, pairs):
        return lax.ppermute(
            value, "owner", [(a * 4 + i, b * 4 + i) for a, b in pairs for i in range(4)]
        )

    def across(value, flip):
        pairs = [
            (r * owners + i, (1 - r) * owners + (i ^ flip)) for r in range(2) for i in range(owners)
        ]
        return lax.ppermute(value, ("replica", "owner"), pairs)

    def to_x(value):
        return across(value, 0)

    def to_y(value):
        return by_owner(value, 2)

    def to_d(value):
        return across(value, 2)

    def to_core(value):
        return by_owner(value, 1)

    def along(unit):
        return [unit] + [by_owner(unit, 4 * s) for s in range(1, planes)]

    def middle(unit):
        return between(unit, [(1, 2), (2, 1)])

    def ends(unit):
        return between(unit, [(1, 0), (2, 3)])

    merged = 1 if planes == 4 else 0
    bf16, f32 = jnp.bfloat16, jnp.float32

    swapped, own, mine, for_x, for_y, for_d = call(
        slices,
        (pltpu.VMEM((rank, quarter), bf16), pltpu.VMEM((rank, quarter + qhalf), bf16))
        + (pltpu.VMEM((rows, quarter + TAG), bf16),) * 4,
        (
            place,
            factor_down,
            factor_up,
            group_variants,
            slot_of,
            row_choice[None, :],
            hidden,
        ),
        scalars=1,
        whole=6,
        scratch=[
            pltpu.SMEM(group_variants.shape, jnp.int32),
            pltpu.SMEM(slot_of.shape, jnp.int32),
            pltpu.VMEM((1, rows), jnp.int32),
            pltpu.SemaphoreType.DMA((10,)),
        ],
    )
    done = {}

    def step(name):
        if name not in done:
            done[name] = None
            waits = [step(w) for w in (ORDER.get(name, ()) if planes == 4 else ())]
            done[name] = steps[name](lambda *v: lax.optimization_barrier((*v, *waits))[: len(v)])
        return done[name]

    def held_up():
        parts = [own, step("A1"), step("A2"), step("A3") + step("A4")]
        return jnp.concatenate([u[:, quarter:] for u in parts], axis=0)

    steps = {
        "P": lambda late: to_y(*late(swapped)),
        "X": lambda late: to_x(*late(for_x)),
        "Y": lambda late: to_y(*late(for_y)),
        "D": lambda late: to_d(*late(for_d)),
        "A1": lambda late: by_owner(*late(own), 4),
        "A2": lambda late: by_owner(*late(own), 8),
        "A3": lambda late: middle(*late(own)),
        "A4": lambda late: ends(*late(step("A2"))),
        "B1": lambda late: by_owner(*late(step("P")), 4),
        "B2": lambda late: by_owner(*late(step("P")), 8),
        "B3": lambda late: middle(*late(step("P"))),
        "B4": lambda late: ends(*late(step("B2"))),
        "base": lambda late: jnp.dot(*late(hidden), base_weight, preferred_element_type=f32),
        "C1": lambda late: to_core(jnp.concatenate(late(mine, step("X")), axis=0)),
        "C2": lambda late: to_core(jnp.concatenate(late(step("Y"), step("D")), axis=0)),
        "U": lambda late: late(held_up())[0],
        "UX": lambda late: to_x(*late(step("U"))),
        "UY": lambda late: to_y(*late(step("U"))),
        "UD": lambda late: to_d(*late(step("U"))),
        "K": lambda late: late(place)[0],
    }
    if merged:
        a_units = [own] + [step(f"A{i}") for i in range(1, 5)]
        b_units = [step("P")] + [step(f"B{i}") for i in range(1, 5)]
        ups = [step("U"), step("UX"), step("UY"), step("UD")]
    else:
        a_units, b_units = along(own), along(step("P"))
        ups = jnp.concatenate([u[:, quarter:] for u in a_units], axis=0)
        ups = [ups, to_x(ups), to_y(ups), to_d(ups)]
    blocks = [mine] + [step(n) for n in ("X", "Y", "D", "C1", "C2")]
    pair, base = step("C1"), step("base")
    first_place = step("K")

    scratch = [pltpu.VMEM((8 * rows, quarter), bf16)]
    flops = 2 * 8 * rows * quarter * planes * rank
    part = call(
        functools.partial(sum_z, False, planes, merged),
        jax.ShapeDtypeStruct((8, rows, 2 * rank), f32),
        (first_place, *blocks, *a_units),
        scalars=1,
        flops=flops,
        scratch=scratch,
    )
    z_here, z_x, z_y, z_d = call(
        functools.partial(sum_z, True, planes, merged),
        (jax.ShapeDtypeStruct((2, rows, 2 * rank), f32),) * 4,
        (place, *blocks, *b_units, part),
        scalars=1,
        flops=flops,
        scratch=scratch,
    )
    here_sum, away = call(
        functools.partial(add_up, planes),
        (jax.ShapeDtypeStruct((rows, qwidth), f32),) * 2,
        (place, base, mine, pair, z_here, to_x(z_x), to_y(z_y), to_d(z_d), *ups),
        scalars=1,
        flops=2 * rows * owners * rank * qwidth,
    )
    return call(
        add, jax.ShapeDtypeStruct((rows, qwidth), bf16), (here_sum, to_core(away)), flops=rows * qwidth
    )


def solution(mesh):
    return jax.shard_map(
        body,
        mesh=mesh,
        in_specs=(
            P(("replica", "owner"), None),
            P(),
            P("owner", None, None),
            P("owner", None, None),
            P(("replica", "owner"), None),
            P(("replica", "owner")),
            P(),
        ),
        out_specs=P(("replica", "owner"), None),
        check_vma=False,
    )
```

```python
import functools

import jax
import jax.numpy as jnp
from jax import lax
from jax.experimental import pallas as pl
from jax.experimental.pallas import tpu as pltpu
from jax.sharding import PartitionSpec as P

TAG = 128
FIRST = ("P", "X", "A2", "A1", "Y")
SECOND = ("A4", "A3", "D")
ORDER = {"D": ("P",)}
ORDER |= dict.fromkeys(("A3", "A4", "B1", "B2", "B3"), FIRST)
ORDER |= dict.fromkeys(("U", "C1", "C2"), SECOND)
VMEM = pl.BlockSpec(memory_space=pltpu.VMEM)
SMEM = pl.BlockSpec(memory_space=pltpu.SMEM)
HBM = pl.BlockSpec(memory_space=pltpu.HBM)


def call(kernel, out, operands, scalars=0, whole=0, flops=0, scratch=()):
    operands = list(operands)
    if whole:
        operands[-whole:] = [
            pltpu.with_memory_space_constraint(o, pltpu.HBM) for o in operands[-whole:]
        ]
    moved = sum(o.size * o.dtype.itemsize for o in operands)
    return pl.pallas_call(
        kernel,
        out_shape=out,
        in_specs=[SMEM] * scalars + [VMEM] * (len(operands) - scalars - whole) + [HBM] * whole,
        out_specs=jax.tree.map(lambda _: VMEM, out),
        scratch_shapes=scratch,
        cost_estimate=pl.CostEstimate(flops=flops, bytes_accessed=moved, transcendentals=0),
        compiler_params=pltpu.CompilerParams(vmem_limit_bytes=(16 if whole else 48) << 20),
    )(*operands)


def slices(place, down, up, hbm_variants, hbm_slots, hbm_choice, hidden, *refs):
    swapped, own, *outs, variants, slot_of, choice, sems = refs
    quarter, qhalf = swapped.shape[1], own.shape[1] - swapped.shape[1]
    rows = outs[0].shape[0]
    x, column = place[0], place[2]

    def columns(part, width):
        return pl.ds(pl.multiple_of(part * width, 128), width)

    parts = (x * 2 + column, (1 - x) * 2 + column, x * 2 + 1 - column, (1 - x) * 2 + 1 - column)
    pairs = [
        (hbm_variants, variants),
        (hbm_slots, slot_of),
        (hbm_choice, choice),
        (down.at[0, :, columns(parts[2], quarter)], swapped),
        (down.at[0, :, columns(parts[0], quarter)], own.at[:, :quarter]),
        (up.at[0, :, columns(x, qhalf)], own.at[:, quarter:]),
    ]
    pairs += [
        (hidden.at[:, columns(part, quarter)], out.at[:, :quarter])
        for part, out in zip(parts, outs)
    ]
    copies = [pltpu.make_async_copy(a, b, sems.at[i]) for i, (a, b) in enumerate(pairs)]
    for copy in copies:
        copy.start()
    for copy in copies[:3]:
        copy.wait()
    slot = jnp.zeros((1, rows), jnp.int32)
    for k in range(variants.shape[1]):
        slot = jnp.where(choice[...] == k, slot_of[variants[0, k]], slot)
    diagonal = lax.broadcasted_iota(jnp.int32, (rows, rows), 0) == lax.broadcasted_iota(
        jnp.int32, (rows, rows), 1
    )
    column = jnp.sum(jnp.where(diagonal, slot.astype(jnp.float32), 0.0), axis=1, keepdims=True)
    tag = jnp.broadcast_to(column, (rows, TAG)).astype(jnp.bfloat16)
    for out in outs:
        out[:, quarter:] = tag
    for copy in copies[3:]:
        copy.wait()


def ids_of(plane, column, core, first, count, rank):
    lane = lax.broadcasted_iota(jnp.int32, (1, count * rank), 1)
    return ((plane ^ (first + lane // rank)) * 4) + column * 2 + core


def sum_z(flipped, units, merged, place, *refs):
    plane, column, core = place[1], place[2], place[3]
    column = 1 - column if flipped else column
    blocks, refs = refs[:6], refs[6:]
    held, refs = refs[: units + merged], refs[units + merged :]
    *refs, hid = refs
    before, outs = (refs[:1], refs[1:]) if flipped else ((), refs)
    rows, quarter = blocks[0].shape[0], blocks[0].shape[1] - TAG
    rank = held[0].shape[0]
    tags = []
    for block in blocks:
        for first in range(0, block.shape[0], rows):
            span = slice(first, first + rows)
            hid[len(tags) * rows : (len(tags) + 1) * rows, :] = block[span, :quarter]
            tag = block[span, quarter : quarter + 1]
            tags.append(tag.astype(jnp.float32).astype(jnp.int32))
    some = min(units, 4)
    sums = [before[0][i] if before else None for i in range(8)]
    for first in range(0, units, some):
        parts = [h[:, :quarter] for h in held[first : first + some]]
        if merged:
            parts[-1] = parts[-1] + held[units][:, :quarter]
        z = lax.dot_general(
            hid[...],
            jnp.concatenate(parts, axis=0),
            (((1,), (1,)), ((), ())),
            preferred_element_type=jnp.float32,
        )
        ids = ids_of(plane, column, core, first, some, rank)
        for i in range(8):
            kept = jnp.where(tags[i] == ids, z[i * rows : (i + 1) * rows, :], 0.0)
            kept = sum(kept[:, j : j + 128] for j in range(0, some * rank, 128))
            sums[i] = kept if sums[i] is None else sums[i] + kept
    for i in range(8):
        if flipped:
            outs[i % 4][i // 4] = sums[i]
        else:
            outs[0][i] = sums[i]


def add_up(planes, place, base, mine, theirs, z_here, z_x, z_y, z_d, *refs):
    *held, out, away = refs
    x, plane, column, core = place[0], place[1], place[2], place[3]
    rows, quarter = mine.shape[0], mine.shape[1] - TAG
    rank = z_here.shape[2] // 2
    qhalf = held[0].shape[1]
    tag = jnp.concatenate(
        [mine[:, quarter : quarter + 1], theirs[:rows, quarter : quarter + 1]], axis=0
    )
    tag = tag.astype(jnp.float32).astype(jnp.int32)
    both = [z_here[i] + z_x[i] + z_y[i] + z_d[i] for i in range(2)]
    z = jnp.concatenate([b[:, :rank] + b[:, rank:] for b in both], axis=0)
    z = z.astype(jnp.bfloat16).astype(jnp.float32)
    some = min(planes, 4)
    spread = jnp.concatenate([z] * some, axis=1)
    near = jnp.zeros((2 * rows, qhalf), jnp.float32)
    far = jnp.zeros((2 * rows, qhalf), jnp.float32)
    for first in range(0, planes, some):
        span = slice(first * rank, (first + some) * rank)
        for y in range(2):
            ids = ids_of(plane, 1 - column if y else column, core, first, some, rank)
            picked = jnp.where(tag == ids, spread, 0.0).astype(jnp.bfloat16)
            near += jnp.dot(picked, held[y * 2][span, :], preferred_element_type=jnp.float32)
            far += jnp.dot(picked, held[y * 2 + 1][span, :], preferred_element_type=jnp.float32)
    for half, value in ((x, near), (1 - x, far)):
        columns = pl.ds(pl.multiple_of(half * qhalf, 128), qhalf)
        out[:, columns] = base[:, columns] + value[:rows]
        away[:, columns] = value[rows:]


def add(here, came, out):
    out[...] = (here[...] + came[...]).astype(out.dtype)


def body(hidden, base_weight, factor_down, factor_up, group_variants, row_choice, slot_of):
    owners = lax.axis_size("owner")
    assert lax.axis_size("replica") == 2 and owners % 4 == 0 and owners <= 256
    planes = owners // 4
    rows, width = hidden.shape
    rank = factor_down.shape[1]
    qwidth = factor_up.shape[2]
    quarter, qhalf = width // 4, qwidth // 2
    here = lax.axis_index("owner")
    place = jnp.stack([lax.axis_index("replica"), here // 4, (here // 2) % 2, here % 2])

    def by_owner(value, flip):
        return lax.ppermute(value, "owner", [(i, i ^ flip) for i in range(owners)])

    def between(value, pairs):
        return lax.ppermute(
            value, "owner", [(a * 4 + i, b * 4 + i) for a, b in pairs for i in range(4)]
        )

    def across(value, flip):
        pairs = [
            (r * owners + i, (1 - r) * owners + (i ^ flip)) for r in range(2) for i in range(owners)
        ]
        return lax.ppermute(value, ("replica", "owner"), pairs)

    def to_x(value):
        return across(value, 0)

    def to_y(value):
        return by_owner(value, 2)

    def to_d(value):
        return across(value, 2)

    def to_core(value):
        return by_owner(value, 1)

    def along(unit):
        return [unit] + [by_owner(unit, 4 * s) for s in range(1, planes)]

    def middle(unit):
        return between(unit, [(1, 2), (2, 1)])

    def ends(unit):
        return between(unit, [(1, 0), (2, 3)])

    merged = 1 if planes == 4 else 0
    bf16, f32 = jnp.bfloat16, jnp.float32

    swapped, own, mine, for_x, for_y, for_d = call(
        slices,
        (pltpu.VMEM((rank, quarter), bf16), pltpu.VMEM((rank, quarter + qhalf), bf16))
        + (pltpu.VMEM((rows, quarter + TAG), bf16),) * 4,
        (
            place,
            factor_down,
            factor_up,
            group_variants,
            slot_of,
            row_choice[None, :],
            hidden,
        ),
        scalars=1,
        whole=6,
        scratch=[
            pltpu.SMEM(group_variants.shape, jnp.int32),
            pltpu.SMEM(slot_of.shape, jnp.int32),
            pltpu.VMEM((1, rows), jnp.int32),
            pltpu.SemaphoreType.DMA((10,)),
        ],
    )
    done = {}

    def step(name):
        if name not in done:
            done[name] = None
            waits = [step(w) for w in (ORDER.get(name, ()) if planes == 4 else ())]
            done[name] = steps[name](lambda *v: lax.optimization_barrier((*v, *waits))[: len(v)])
        return done[name]

    def held_up():
        parts = [own, step("A1"), step("A2"), step("A3") + step("A4")]
        return jnp.concatenate([u[:, quarter:] for u in parts], axis=0)

    steps = {
        "P": lambda late: to_y(*late(swapped)),
        "X": lambda late: to_x(*late(for_x)),
        "Y": lambda late: to_y(*late(for_y)),
        "D": lambda late: to_d(*late(for_d)),
        "A1": lambda late: by_owner(*late(own), 4),
        "A2": lambda late: by_owner(*late(own), 8),
        "A3": lambda late: middle(*late(own)),
        "A4": lambda late: ends(*late(step("A2"))),
        "B1": lambda late: by_owner(*late(step("P")), 4),
        "B2": lambda late: by_owner(*late(step("P")), 8),
        "B3": lambda late: by_owner(*late(step("P")), 12),
        "base": lambda late: jnp.dot(*late(hidden), base_weight, preferred_element_type=f32),
        "C1": lambda late: to_core(jnp.concatenate(late(mine, step("X")), axis=0)),
        "C2": lambda late: to_core(jnp.concatenate(late(step("Y"), step("D")), axis=0)),
        "U": lambda late: late(held_up())[0],
        "UX": lambda late: to_x(*late(step("U"))),
        "UY": lambda late: to_y(*late(step("U"))),
        "UD": lambda late: to_d(*late(step("U"))),
        "K": lambda late: late(place)[0],
    }
    if merged:
        a_units = [own] + [step(f"A{i}") for i in range(1, 5)]
        b_units = [step("P")] + [step(f"B{i}") for i in range(1, 4)]
        ups = [step("U"), step("UX"), step("UY"), step("UD")]
    else:
        a_units, b_units = along(own), along(step("P"))
        ups = jnp.concatenate([u[:, quarter:] for u in a_units], axis=0)
        ups = [ups, to_x(ups), to_y(ups), to_d(ups)]
    blocks = [mine] + [step(n) for n in ("X", "Y", "D", "C1", "C2")]
    pair, base = step("C1"), step("base")
    first_place = step("K")

    scratch = [pltpu.VMEM((8 * rows, quarter), bf16)]
    flops = 2 * 8 * rows * quarter * planes * rank
    part = call(
        functools.partial(sum_z, False, planes, merged),
        jax.ShapeDtypeStruct((8, rows, 2 * rank), f32),
        (first_place, *blocks, *a_units),
        scalars=1,
        flops=flops,
        scratch=scratch,
    )
    z_here, z_x, z_y, z_d = call(
        functools.partial(sum_z, True, planes, 0),
        (jax.ShapeDtypeStruct((2, rows, 2 * rank), f32),) * 4,
        (place, *blocks, *b_units, part),
        scalars=1,
        flops=flops,
        scratch=scratch,
    )
    here_sum, away = call(
        functools.partial(add_up, planes),
        (jax.ShapeDtypeStruct((rows, qwidth), f32),) * 2,
        (place, base, mine, pair, z_here, to_x(z_x), to_y(z_y), to_d(z_d), *ups),
        scalars=1,
        flops=2 * rows * owners * rank * qwidth,
    )
    return call(
        add, jax.ShapeDtypeStruct((rows, qwidth), bf16), (here_sum, to_core(away)), flops=rows * qwidth
    )


def solution(mesh):
    return jax.shard_map(
        body,
        mesh=mesh,
        in_specs=(
            P(("replica", "owner"), None),
            P(),
            P("owner", None, None),
            P("owner", None, None),
            P(("replica", "owner"), None),
            P(("replica", "owner")),
            P(),
        ),
        out_specs=P(("replica", "owner"), None),
        check_vma=False,
    )
```

```python
import functools

import jax
import jax.numpy as jnp
from jax import lax
from jax.experimental import pallas as pl
from jax.experimental.pallas import tpu as pltpu
from jax.sharding import PartitionSpec as P

TAG = 128
ORDER = {
    "Y": ("A1",),
    "A3": ("A1", "P"),
    "D": ("X", "P"),
    "B1": ("A3",),
    "B3": ("A3",),
    "U": ("A3", "D"),
    "C1": ("A3", "A4", "B2", "D"),
    "C2": ("A3", "A4", "B2", "D"),
}
VMEM = pl.BlockSpec(memory_space=pltpu.VMEM)
SMEM = pl.BlockSpec(memory_space=pltpu.SMEM)
HBM = pl.BlockSpec(memory_space=pltpu.HBM)


def call(kernel, out, operands, scalars=0, whole=0, flops=0, scratch=()):
    operands = list(operands)
    if whole:
        operands[-whole:] = [
            pltpu.with_memory_space_constraint(o, pltpu.HBM) for o in operands[-whole:]
        ]
    moved = sum(o.size * o.dtype.itemsize for o in operands)
    return pl.pallas_call(
        kernel,
        out_shape=out,
        in_specs=[SMEM] * scalars + [VMEM] * (len(operands) - scalars - whole) + [HBM] * whole,
        out_specs=jax.tree.map(lambda _: VMEM, out),
        scratch_shapes=scratch,
        cost_estimate=pl.CostEstimate(flops=flops, bytes_accessed=moved, transcendentals=0),
        compiler_params=pltpu.CompilerParams(vmem_limit_bytes=(16 if whole else 48) << 20),
    )(*operands)


def slices(place, down, up, hbm_variants, hbm_slots, hbm_choice, hidden, *refs):
    swapped, own, *outs, variants, slot_of, choice, sems = refs
    quarter, qhalf = swapped.shape[1], own.shape[1] - swapped.shape[1]
    rows = outs[0].shape[0]
    x, column = place[0], place[2]

    def columns(part, width):
        return pl.ds(pl.multiple_of(part * width, 128), width)

    parts = (x * 2 + column, (1 - x) * 2 + column, x * 2 + 1 - column, (1 - x) * 2 + 1 - column)
    pairs = [
        (hbm_variants, variants),
        (hbm_slots, slot_of),
        (hbm_choice, choice),
        (down.at[0, :, columns(parts[2], quarter)], swapped),
        (down.at[0, :, columns(parts[0], quarter)], own.at[:, :quarter]),
        (up.at[0, :, columns(x, qhalf)], own.at[:, quarter:]),
    ]
    pairs += [
        (hidden.at[:, columns(part, quarter)], out.at[:, :quarter])
        for part, out in zip(parts, outs)
    ]
    copies = [pltpu.make_async_copy(a, b, sems.at[i]) for i, (a, b) in enumerate(pairs)]
    for copy in copies:
        copy.start()
    for copy in copies[:3]:
        copy.wait()
    slot = jnp.zeros((1, rows), jnp.int32)
    for k in range(variants.shape[1]):
        slot = jnp.where(choice[...] == k, slot_of[variants[0, k]], slot)
    diagonal = lax.broadcasted_iota(jnp.int32, (rows, rows), 0) == lax.broadcasted_iota(
        jnp.int32, (rows, rows), 1
    )
    column = jnp.sum(jnp.where(diagonal, slot.astype(jnp.float32), 0.0), axis=1, keepdims=True)
    tag = jnp.broadcast_to(column, (rows, TAG)).astype(jnp.bfloat16)
    for out in outs:
        out[:, quarter:] = tag
    for copy in copies[3:]:
        copy.wait()


def ids_of(plane, column, core, first, count, rank):
    lane = lax.broadcasted_iota(jnp.int32, (1, count * rank), 1)
    return ((plane ^ (first + lane // rank)) * 4) + column * 2 + core


def sum_z(flipped, units, merged, place, *refs):
    plane, column, core = place[1], place[2], place[3]
    column = 1 - column if flipped else column
    blocks, refs = refs[:6], refs[6:]
    held, refs = refs[: units + merged], refs[units + merged :]
    *refs, hid = refs
    before, outs = (refs[:1], refs[1:]) if flipped else ((), refs)
    rows, quarter = blocks[0].shape[0], blocks[0].shape[1] - TAG
    rank = held[0].shape[0]
    tags = []
    for block in blocks:
        for first in range(0, block.shape[0], rows):
            span = slice(first, first + rows)
            hid[len(tags) * rows : (len(tags) + 1) * rows, :] = block[span, :quarter]
            tag = block[span, quarter : quarter + 1]
            tags.append(tag.astype(jnp.float32).astype(jnp.int32))
    some = min(units, 4)
    sums = [before[0][i] if before else None for i in range(8)]
    for first in range(0, units, some):
        parts = [h[:, :quarter] for h in held[first : first + some]]
        if merged:
            parts[-1] = parts[-1] + held[units][:, :quarter]
        z = lax.dot_general(
            hid[...],
            jnp.concatenate(parts, axis=0),
            (((1,), (1,)), ((), ())),
            preferred_element_type=jnp.float32,
        )
        ids = ids_of(plane, column, core, first, some, rank)
        for i in range(8):
            kept = jnp.where(tags[i] == ids, z[i * rows : (i + 1) * rows, :], 0.0)
            kept = sum(kept[:, j : j + 128] for j in range(0, some * rank, 128))
            sums[i] = kept if sums[i] is None else sums[i] + kept
    for i in range(8):
        if flipped:
            outs[i % 4][i // 4] = sums[i]
        else:
            outs[0][i] = sums[i]


def add_up(planes, place, base, mine, theirs, z_here, z_x, z_y, z_d, *refs):
    *held, out, away = refs
    x, plane, column, core = place[0], place[1], place[2], place[3]
    rows, quarter = mine.shape[0], mine.shape[1] - TAG
    rank = z_here.shape[2] // 2
    qhalf = held[0].shape[1]
    tag = jnp.concatenate(
        [mine[:, quarter : quarter + 1], theirs[:rows, quarter : quarter + 1]], axis=0
    )
    tag = tag.astype(jnp.float32).astype(jnp.int32)
    both = [z_here[i] + z_x[i] + z_y[i] + z_d[i] for i in range(2)]
    z = jnp.concatenate([b[:, :rank] + b[:, rank:] for b in both], axis=0)
    z = z.astype(jnp.bfloat16).astype(jnp.float32)
    some = min(planes, 4)
    spread = jnp.concatenate([z] * some, axis=1)
    near = jnp.zeros((2 * rows, qhalf), jnp.float32)
    far = jnp.zeros((2 * rows, qhalf), jnp.float32)
    for first in range(0, planes, some):
        span = slice(first * rank, (first + some) * rank)
        for y in range(2):
            ids = ids_of(plane, 1 - column if y else column, core, first, some, rank)
            picked = jnp.where(tag == ids, spread, 0.0).astype(jnp.bfloat16)
            near += jnp.dot(picked, held[y * 2][span, :], preferred_element_type=jnp.float32)
            far += jnp.dot(picked, held[y * 2 + 1][span, :], preferred_element_type=jnp.float32)
    for half, value in ((x, near), (1 - x, far)):
        columns = pl.ds(pl.multiple_of(half * qhalf, 128), qhalf)
        out[:, columns] = base[:, columns] + value[:rows]
        away[:, columns] = value[rows:]


def add(here, came, out):
    out[...] = (here[...] + came[...]).astype(out.dtype)


def body(hidden, base_weight, factor_down, factor_up, group_variants, row_choice, slot_of):
    owners = lax.axis_size("owner")
    assert lax.axis_size("replica") == 2 and owners % 4 == 0 and owners <= 256
    planes = owners // 4
    rows, width = hidden.shape
    rank = factor_down.shape[1]
    qwidth = factor_up.shape[2]
    quarter, qhalf = width // 4, qwidth // 2
    here = lax.axis_index("owner")
    place = jnp.stack([lax.axis_index("replica"), here // 4, (here // 2) % 2, here % 2])

    def by_owner(value, flip):
        return lax.ppermute(value, "owner", [(i, i ^ flip) for i in range(owners)])

    def between(value, pairs):
        return lax.ppermute(
            value, "owner", [(a * 4 + i, b * 4 + i) for a, b in pairs for i in range(4)]
        )

    def across(value, flip):
        pairs = [
            (r * owners + i, (1 - r) * owners + (i ^ flip)) for r in range(2) for i in range(owners)
        ]
        return lax.ppermute(value, ("replica", "owner"), pairs)

    def to_x(value):
        return across(value, 0)

    def to_y(value):
        return by_owner(value, 2)

    def to_d(value):
        return across(value, 2)

    def to_core(value):
        return by_owner(value, 1)

    def along(unit):
        return [unit] + [by_owner(unit, 4 * s) for s in range(1, planes)]

    def middle(unit):
        return between(unit, [(1, 2), (2, 1)])

    def ends(unit):
        return between(unit, [(1, 0), (2, 3)])

    merged = 1 if planes == 4 else 0
    bf16, f32 = jnp.bfloat16, jnp.float32

    swapped, own, mine, for_x, for_y, for_d = call(
        slices,
        (pltpu.VMEM((rank, quarter), bf16), pltpu.VMEM((rank, quarter + qhalf), bf16))
        + (pltpu.VMEM((rows, quarter + TAG), bf16),) * 4,
        (
            place,
            factor_down,
            factor_up,
            group_variants,
            slot_of,
            row_choice[None, :],
            hidden,
        ),
        scalars=1,
        whole=6,
        scratch=[
            pltpu.SMEM(group_variants.shape, jnp.int32),
            pltpu.SMEM(slot_of.shape, jnp.int32),
            pltpu.VMEM((1, rows), jnp.int32),
            pltpu.SemaphoreType.DMA((10,)),
        ],
    )
    done = {}

    def step(name):
        if name not in done:
            done[name] = None
            waits = [step(w) for w in (ORDER.get(name, ()) if planes == 4 else ())]
            done[name] = steps[name](lambda *v: lax.optimization_barrier((*v, *waits))[: len(v)])
        return done[name]

    def held_up():
        parts = [own, step("A1"), step("A2"), step("A3") + step("A4")]
        return jnp.concatenate([u[:, quarter:] for u in parts], axis=0)

    steps = {
        "P": lambda late: to_y(*late(swapped)),
        "X": lambda late: to_x(*late(for_x)),
        "Y": lambda late: to_y(*late(for_y)),
        "D": lambda late: to_d(*late(for_d)),
        "A1": lambda late: by_owner(*late(own), 4),
        "A2": lambda late: by_owner(*late(own), 8),
        "A3": lambda late: middle(*late(own)),
        "A4": lambda late: ends(*late(step("A2"))),
        "B1": lambda late: by_owner(*late(step("P")), 4),
        "B2": lambda late: by_owner(*late(step("P")), 8),
        "B3": lambda late: by_owner(*late(step("P")), 12),
        "base": lambda late: jnp.dot(*late(hidden), base_weight, preferred_element_type=f32),
        "C1": lambda late: to_core(jnp.concatenate(late(mine, step("X")), axis=0)),
        "C2": lambda late: to_core(jnp.concatenate(late(step("Y"), step("D")), axis=0)),
        "U": lambda late: late(held_up())[0],
        "UX": lambda late: to_x(*late(step("U"))),
        "UY": lambda late: to_y(*late(step("U"))),
        "UD": lambda late: to_d(*late(step("U"))),
        "K": lambda late: late(place)[0],
    }
    if merged:
        a_units = [own] + [step(f"A{i}") for i in range(1, 5)]
        b_units = [step("P")] + [step(f"B{i}") for i in range(1, 4)]
        ups = [step("U"), step("UX"), step("UY"), step("UD")]
    else:
        a_units, b_units = along(own), along(step("P"))
        ups = jnp.concatenate([u[:, quarter:] for u in a_units], axis=0)
        ups = [ups, to_x(ups), to_y(ups), to_d(ups)]
    blocks = [mine] + [step(n) for n in ("X", "Y", "D", "C1", "C2")]
    pair, base = step("C1"), step("base")
    first_place = step("K")

    scratch = [pltpu.VMEM((8 * rows, quarter), bf16)]
    flops = 2 * 8 * rows * quarter * planes * rank
    part = call(
        functools.partial(sum_z, False, planes, merged),
        jax.ShapeDtypeStruct((8, rows, 2 * rank), f32),
        (first_place, *blocks, *a_units),
        scalars=1,
        flops=flops,
        scratch=scratch,
    )
    z_here, z_x, z_y, z_d = call(
        functools.partial(sum_z, True, planes, 0),
        (jax.ShapeDtypeStruct((2, rows, 2 * rank), f32),) * 4,
        (place, *blocks, *b_units, part),
        scalars=1,
        flops=flops,
        scratch=scratch,
    )
    here_sum, away = call(
        functools.partial(add_up, planes),
        (jax.ShapeDtypeStruct((rows, qwidth), f32),) * 2,
        (place, base, mine, pair, z_here, to_x(z_x), to_y(z_y), to_d(z_d), *ups),
        scalars=1,
        flops=2 * rows * owners * rank * qwidth,
    )
    return call(
        add, jax.ShapeDtypeStruct((rows, qwidth), bf16), (here_sum, to_core(away)), flops=rows * qwidth
    )


def solution(mesh):
    return jax.shard_map(
        body,
        mesh=mesh,
        in_specs=(
            P(("replica", "owner"), None),
            P(),
            P("owner", None, None),
            P("owner", None, None),
            P(("replica", "owner"), None),
            P(("replica", "owner")),
            P(),
        ),
        out_specs=P(("replica", "owner"), None),
        check_vma=False,
    )
```

```python
import functools

import jax
import jax.numpy as jnp
from jax import lax
from jax.experimental import pallas as pl
from jax.experimental.pallas import tpu as pltpu
from jax.sharding import PartitionSpec as P

TAG = 128
ORDER = {
    "Y": ("A1",),
    "A3": ("A1", "P"),
    "D": ("X", "P"),
    "B1": ("A3",),
    "B3": ("A3",),
    "U": ("A3", "D"),
    "C1": ("A3", "A4", "B2", "D"),
    "C2": ("A3", "A4", "B2", "D"),
}
VMEM = pl.BlockSpec(memory_space=pltpu.VMEM)
SMEM = pl.BlockSpec(memory_space=pltpu.SMEM)
HBM = pl.BlockSpec(memory_space=pltpu.HBM)


def call(kernel, out, operands, scalars=0, whole=0, flops=0, scratch=()):
    operands = list(operands)
    if whole:
        operands[-whole:] = [
            pltpu.with_memory_space_constraint(o, pltpu.HBM) for o in operands[-whole:]
        ]
    moved = sum(o.size * o.dtype.itemsize for o in operands)
    return pl.pallas_call(
        kernel,
        out_shape=out,
        in_specs=[SMEM] * scalars + [VMEM] * (len(operands) - scalars - whole) + [HBM] * whole,
        out_specs=jax.tree.map(lambda _: VMEM, out),
        scratch_shapes=scratch,
        cost_estimate=pl.CostEstimate(flops=flops, bytes_accessed=moved, transcendentals=0),
        compiler_params=pltpu.CompilerParams(vmem_limit_bytes=(16 if whole else 32) << 20),
    )(*operands)


def slices(place, down, up, hbm_variants, hbm_slots, hbm_choice, hidden, *refs):
    swapped, own, *outs, variants, slot_of, choice, sems = refs
    quarter, qhalf = swapped.shape[1], own.shape[1] - swapped.shape[1]
    rows = outs[0].shape[0]
    x, column = place[0], place[2]

    def columns(part, width):
        return pl.ds(pl.multiple_of(part * width, 128), width)

    parts = (x * 2 + column, (1 - x) * 2 + column, x * 2 + 1 - column, (1 - x) * 2 + 1 - column)
    pairs = [
        (hbm_variants, variants),
        (hbm_slots, slot_of),
        (hbm_choice, choice),
        (down.at[0, :, columns(parts[2], quarter)], swapped),
        (down.at[0, :, columns(parts[0], quarter)], own.at[:, :quarter]),
        (up.at[0, :, columns(x, qhalf)], own.at[:, quarter:]),
    ]
    pairs += [
        (hidden.at[:, columns(part, quarter)], out.at[:, :quarter])
        for part, out in zip(parts, outs)
    ]
    copies = [pltpu.make_async_copy(a, b, sems.at[i]) for i, (a, b) in enumerate(pairs)]
    for copy in copies:
        copy.start()
    for copy in copies[:3]:
        copy.wait()
    slot = jnp.zeros((1, rows), jnp.int32)
    for k in range(variants.shape[1]):
        slot = jnp.where(choice[...] == k, slot_of[variants[0, k]], slot)
    diagonal = lax.broadcasted_iota(jnp.int32, (rows, rows), 0) == lax.broadcasted_iota(
        jnp.int32, (rows, rows), 1
    )
    column = jnp.sum(jnp.where(diagonal, slot.astype(jnp.float32), 0.0), axis=1, keepdims=True)
    tag = jnp.broadcast_to(column, (rows, TAG)).astype(jnp.bfloat16)
    for out in outs:
        out[:, quarter:] = tag
    for copy in copies[3:]:
        copy.wait()


def ids_of(plane, column, core, first, count, rank):
    lane = lax.broadcasted_iota(jnp.int32, (1, count * rank), 1)
    return ((plane ^ (first + lane // rank)) * 4) + column * 2 + core


def sum_z(flipped, units, merged, place, *refs):
    plane, column, core = place[1], place[2], place[3]
    column = 1 - column if flipped else column
    blocks, refs = refs[:6], refs[6:]
    held, refs = refs[: units + merged], refs[units + merged :]
    *refs, hid = refs
    before, outs = (refs[:1], refs[1:]) if flipped else ((), refs)
    rows, quarter = blocks[0].shape[0], blocks[0].shape[1] - TAG
    rank = held[0].shape[0]
    tags = []
    for block in blocks:
        for first in range(0, block.shape[0], rows):
            span = slice(first, first + rows)
            hid[len(tags) * rows : (len(tags) + 1) * rows, :] = block[span, :quarter]
            tag = block[span, quarter : quarter + 1]
            tags.append(tag.astype(jnp.float32).astype(jnp.int32))
    some = min(units, 4)
    sums = [before[0][i] if before else None for i in range(8)]
    for first in range(0, units, some):
        parts = [h[:, :quarter] for h in held[first : first + some]]
        if merged:
            parts[-1] = parts[-1] + held[units][:, :quarter]
        z = lax.dot_general(
            hid[...],
            jnp.concatenate(parts, axis=0),
            (((1,), (1,)), ((), ())),
            preferred_element_type=jnp.float32,
        )
        ids = ids_of(plane, column, core, first, some, rank)
        for i in range(8):
            kept = jnp.where(tags[i] == ids, z[i * rows : (i + 1) * rows, :], 0.0)
            kept = sum(kept[:, j : j + 128] for j in range(0, some * rank, 128))
            sums[i] = kept if sums[i] is None else sums[i] + kept
    if not flipped:
        for i in range(8):
            outs[0][i] = sums[i]
        return
    sums = [v[:, :rank] + v[:, rank:] for v in sums]
    for i in range(4):
        outs[i][...] = jnp.concatenate([sums[i], sums[i + 4]], axis=1)


def add_up(planes, place, base, mine, theirs, z_here, z_x, z_y, z_d, *refs):
    *held, out, away = refs
    x, plane, column, core = place[0], place[1], place[2], place[3]
    rows, quarter = mine.shape[0], mine.shape[1] - TAG
    rank = z_here.shape[1] // 2
    qhalf = held[0].shape[1]
    tag = jnp.concatenate(
        [mine[:, quarter : quarter + 1], theirs[:rows, quarter : quarter + 1]], axis=0
    )
    tag = tag.astype(jnp.float32).astype(jnp.int32)
    both = z_here[...] + z_x[...] + z_y[...] + z_d[...]
    z = jnp.concatenate([both[:, :rank], both[:, rank:]], axis=0)
    z = z.astype(jnp.bfloat16).astype(jnp.float32)
    some = min(planes, 4)
    spread = jnp.concatenate([z] * some, axis=1)
    near = jnp.zeros((2 * rows, qhalf), jnp.float32)
    far = jnp.zeros((2 * rows, qhalf), jnp.float32)
    for first in range(0, planes, some):
        span = slice(first * rank, (first + some) * rank)
        for y in range(2):
            ids = ids_of(plane, 1 - column if y else column, core, first, some, rank)
            picked = jnp.where(tag == ids, spread, 0.0).astype(jnp.bfloat16)
            near += jnp.dot(picked, held[y * 2][span, :], preferred_element_type=jnp.float32)
            far += jnp.dot(picked, held[y * 2 + 1][span, :], preferred_element_type=jnp.float32)
    for half, value in ((x, near), (1 - x, far)):
        columns = pl.ds(pl.multiple_of(half * qhalf, 128), qhalf)
        out[:, columns] = base[:, columns] + value[:rows]
        away[:, columns] = value[rows:]


def add(here, came, out):
    out[...] = (here[...] + came[...]).astype(out.dtype)


def body(hidden, base_weight, factor_down, factor_up, group_variants, row_choice, slot_of):
    owners = lax.axis_size("owner")
    assert lax.axis_size("replica") == 2 and owners % 4 == 0 and owners <= 256
    planes = owners // 4
    rows, width = hidden.shape
    rank = factor_down.shape[1]
    qwidth = factor_up.shape[2]
    quarter, qhalf = width // 4, qwidth // 2
    here = lax.axis_index("owner")
    place = jnp.stack([lax.axis_index("replica"), here // 4, (here // 2) % 2, here % 2])

    def by_owner(value, flip):
        return lax.ppermute(value, "owner", [(i, i ^ flip) for i in range(owners)])

    def between(value, pairs):
        return lax.ppermute(
            value, "owner", [(a * 4 + i, b * 4 + i) for a, b in pairs for i in range(4)]
        )

    def across(value, flip):
        pairs = [
            (r * owners + i, (1 - r) * owners + (i ^ flip)) for r in range(2) for i in range(owners)
        ]
        return lax.ppermute(value, ("replica", "owner"), pairs)

    def to_x(value):
        return across(value, 0)

    def to_y(value):
        return by_owner(value, 2)

    def to_d(value):
        return across(value, 2)

    def to_core(value):
        return by_owner(value, 1)

    def along(unit):
        return [unit] + [by_owner(unit, 4 * s) for s in range(1, planes)]

    def middle(unit):
        return between(unit, [(1, 2), (2, 1)])

    def ends(unit):
        return between(unit, [(1, 0), (2, 3)])

    merged = 1 if planes == 4 else 0
    bf16, f32 = jnp.bfloat16, jnp.float32

    swapped, own, mine, for_x, for_y, for_d = call(
        slices,
        (pltpu.VMEM((rank, quarter), bf16), pltpu.VMEM((rank, quarter + qhalf), bf16))
        + (pltpu.VMEM((rows, quarter + TAG), bf16),) * 4,
        (
            place,
            factor_down,
            factor_up,
            group_variants,
            slot_of,
            row_choice[None, :],
            hidden,
        ),
        scalars=1,
        whole=6,
        scratch=[
            pltpu.SMEM(group_variants.shape, jnp.int32),
            pltpu.SMEM(slot_of.shape, jnp.int32),
            pltpu.VMEM((1, rows), jnp.int32),
            pltpu.SemaphoreType.DMA((10,)),
        ],
    )
    done = {}

    def step(name):
        if name not in done:
            done[name] = None
            waits = [step(w) for w in (ORDER.get(name, ()) if planes == 4 else ())]
            done[name] = steps[name](lambda *v: lax.optimization_barrier((*v, *waits))[: len(v)])
        return done[name]

    def held_up():
        parts = [own, step("A1"), step("A2"), step("A3") + step("A4")]
        return jnp.concatenate([u[:, quarter:] for u in parts], axis=0)

    steps = {
        "P": lambda late: to_y(*late(swapped)),
        "X": lambda late: to_x(*late(for_x)),
        "Y": lambda late: to_y(*late(for_y)),
        "D": lambda late: to_d(*late(for_d)),
        "A1": lambda late: by_owner(*late(own), 4),
        "A2": lambda late: by_owner(*late(own), 8),
        "A3": lambda late: middle(*late(own)),
        "A4": lambda late: ends(*late(step("A2"))),
        "B1": lambda late: by_owner(*late(step("P")), 4),
        "B2": lambda late: by_owner(*late(step("P")), 8),
        "B3": lambda late: by_owner(*late(step("P")), 12),
        "base": lambda late: jnp.dot(*late(hidden), base_weight, preferred_element_type=f32),
        "C1": lambda late: to_core(jnp.concatenate(late(mine, step("X")), axis=0)),
        "C2": lambda late: to_core(jnp.concatenate(late(step("Y"), step("D")), axis=0)),
        "U": lambda late: late(held_up())[0],
        "UX": lambda late: to_x(*late(step("U"))),
        "UY": lambda late: to_y(*late(step("U"))),
        "UD": lambda late: to_d(*late(step("U"))),
        "K": lambda late: late(place)[0],
    }
    if merged:
        a_units = [own] + [step(f"A{i}") for i in range(1, 5)]
        b_units = [step("P")] + [step(f"B{i}") for i in range(1, 4)]
        ups = [step("U"), step("UX"), step("UY"), step("UD")]
    else:
        a_units, b_units = along(own), along(step("P"))
        ups = jnp.concatenate([u[:, quarter:] for u in a_units], axis=0)
        ups = [ups, to_x(ups), to_y(ups), to_d(ups)]
    blocks = [mine] + [step(n) for n in ("X", "Y", "D", "C1", "C2")]
    pair, base = step("C1"), step("base")
    first_place = step("K")

    scratch = [pltpu.VMEM((8 * rows, quarter), bf16)]
    flops = 2 * 8 * rows * quarter * planes * rank
    part = call(
        functools.partial(sum_z, False, planes, merged),
        jax.ShapeDtypeStruct((8, rows, 2 * rank), f32),
        (first_place, *blocks, *a_units),
        scalars=1,
        flops=flops,
        scratch=scratch,
    )
    z_here, z_x, z_y, z_d = call(
        functools.partial(sum_z, True, planes, 0),
        (jax.ShapeDtypeStruct((rows, 2 * rank), f32),) * 4,
        (place, *blocks, *b_units, part),
        scalars=1,
        flops=flops,
        scratch=scratch,
    )
    here_sum, away = call(
        functools.partial(add_up, planes),
        (jax.ShapeDtypeStruct((rows, qwidth), f32),) * 2,
        (place, base, mine, pair, z_here, to_x(z_x), to_y(z_y), to_d(z_d), *ups),
        scalars=1,
        flops=2 * rows * owners * rank * qwidth,
    )
    return call(
        add, jax.ShapeDtypeStruct((rows, qwidth), bf16), (here_sum, to_core(away)), flops=rows * qwidth
    )


def solution(mesh):
    return jax.shard_map(
        body,
        mesh=mesh,
        in_specs=(
            P(("replica", "owner"), None),
            P(),
            P("owner", None, None),
            P("owner", None, None),
            P(("replica", "owner"), None),
            P(("replica", "owner")),
            P(),
        ),
        out_specs=P(("replica", "owner"), None),
        check_vma=False,
    )
```
